128 devices in a mesh: row: 16 (over z_lo, y, core), col: 8 (over x, z_hi).
Axes of the slice: x: 4, y: 4, z: 4 (z_hi: 2, z_lo: 2; z = z_hi * 2 + z_lo), core: 2. Of those that a mesh axis runs over, the one named last changes fastest.
Arguments:
- coeffs: float32 [16, 8, 8, 8, 64, 512], P('row', 'col'), may hold values from -6 to 6
- row_weights: float32 [3, 16, 8, 8, 8, 64, 128], P(None, 'row', 'col'), may hold values from -0.5 to 0.5
- col_weights: float32 [3, 16, 8, 8, 8, 64, 128], P(None, 'row', 'col'), may hold values from -0.5 to 0.5
Outputs:
- result: float32 [16, 8, 8, 8, 64, 512], P('row', 'col')
The draws below stay inside these ranges and needn't reach their ends.
All inputs are finite; a program needn't handle non-finite values.
Results may differ from the reference program's by a relative error of at most 0.00013.
Values sent between devices are 32-bit elements; how exact they have to be, the bound alone decides.
A program may use at most 128 MiB of HBM per device.

```python
import jax
import jax.numpy as jnp
from jax import lax

R = 64
S = 512
TAIL = 8
RL = 3
CL = 3
BR = 16
BC = 8


def level_of(stream_key, extent, cuts, smallest, top_value):
    def one(dim, shards_of):
        draws = jax.random.uniform(jax.random.fold_in(jax.random.fold_in(stream_key, 6), dim), (shards_of,), jnp.float32, smallest / len(cuts), top_value / len(cuts))
        return jnp.repeat(jnp.exp(draws), extent[dim] // shards_of).reshape((-1,) + (1,) * (len(extent) - dim - 1))

    loudness = one(*cuts[0])
    for cut in cuts[1:]:
        loudness = loudness * one(*cut)
    return loudness


def scatter_about(own_key, shape, spread, bound, pieces=(), dtype=jnp.bfloat16):
    gain = level_of(own_key, shape, pieces, -0.22, 0.18) if pieces else 1.0
    result = jax.random.normal(own_key, shape, jnp.float32) * spread * gain
    return jnp.minimum(jnp.maximum(result, -bound), bound).astype(dtype)


def setup_inputs(seed: int = 0) -> dict:
    seeds = jax.random.split(jax.random.key(seed), 4)
    coeffs = scatter_about(seeds[0], (BR, BC, BC, TAIL, R, S), 1.0, 6.0, ((0, 16), (1, 8)), jnp.float32)
    row_weights = scatter_about(seeds[1], (RL, BR, BC, BC, TAIL, R, 2 * R), (2 * R) ** -0.5, 0.5, ((1, 16), (2, 8)), jnp.float32)
    col_weights = scatter_about(seeds[2], (CL, BR, BC, BC, TAIL, R, 2 * R), (2 * R) ** -0.5, 0.5, ((1, 16), (2, 8)), jnp.float32)
    return {"coeffs": coeffs, "row_weights": row_weights, "col_weights": col_weights}


def flip_axis(values, axis, stride):
    shape = values.shape
    split = shape[:axis] + (shape[axis] // (2 * stride), 2, stride) + shape[axis + 1:]
    return jnp.flip(values.reshape(split), axis=axis + 1).reshape(shape)


def mix_level(weights, state, partner):
    joined = jnp.concatenate([state, partner], axis=-2)
    return jnp.einsum("...xy,...ys->...xs", weights, joined, precision=lax.Precision.HIGHEST)


def reference(coeffs, row_weights, col_weights):
    state = coeffs
    for level in range(RL):
        stride = BR >> (level + 1)
        state = mix_level(row_weights[level], state, flip_axis(state, 0, stride))
    state = jnp.transpose(state, (0, 2, 1, 3, 4, 5))
    span = BC * TAIL
    shaped = state.reshape(BR, BC, span, R, S)
    for level in range(CL):
        stride = span >> (level + 1)
        weights = col_weights[level].reshape(BR, BC, span, R, 2 * R)
        shaped = mix_level(weights, shaped, flip_axis(shaped, 2, stride))
    return shaped.reshape(BR, BC, BC, TAIL, R, S)
```

```python
import jax
import jax.numpy as jnp
from jax import lax
from jax.experimental import pallas as pl
from jax.experimental.pallas import tpu as pltpu
from jax.sharding import PartitionSpec as P

MESH = pl.DeviceIdType.MESH
GROUP = 8
TAIL = 8
R = 64
S = 512
HALF = 256
LEVELS = 3


def split(value):
    high = value.astype(jnp.bfloat16)
    low = (value - high.astype(jnp.float32)).astype(jnp.bfloat16)
    return high, low


def dot(left, right):
    return jnp.dot(left, right, preferred_element_type=jnp.float32)


def mix_pair(weights, state, a, b):
    top = weights[a]
    bottom = pltpu.roll(weights[b], R, 1)
    wh, wl = split(jnp.concatenate([top, bottom], axis=0))
    for n in range(0, S, HALF):
        cols = pl.ds(n, HALF)
        xh, xl = split(jnp.concatenate([state[a, :, cols], state[b, :, cols]], axis=0))
        y = dot(wh, xh) + dot(wh, xl) + dot(wl, xh)
        state[a, :, cols] = y[:R]
        state[b, :, cols] = y[R:]


def mix_levels(weights, state):
    for level in range(LEVELS):
        stride = GROUP >> level + 1
        for a in range(GROUP):
            if not a & stride:
                mix_pair(weights.at[level], state, a, a | stride)


def kernel(x_ref, rw_ref, cw_ref, out_ref, xb, wb, zb, cb, xsem, wsem, zsem, csem, osem, ssem, vsem):
    row, col = lax.axis_index("row"), lax.axis_index("col")
    me, core = row // 2, row % 2

    barrier = pltpu.get_barrier_semaphore()

    def greet(step, carry):
        there = (2 * ((me + step // GROUP) % GROUP) + core, (col + step) % GROUP)
        pl.semaphore_signal(barrier, 1, device_id=there, device_id_type=MESH)
        return carry

    lax.fori_loop(1, GROUP * GROUP, greet, 0)
    pl.semaphore_wait(barrier, GROUP * GROUP - 1)

    def send_first(t, carry):
        for step in range(GROUP):
            a = (me + step) % GROUP
            block = ((a + col + t) % GROUP) * TAIL + t
            if step == 0:
                pltpu.make_async_copy(x_ref.at[block], xb.at[t, me], xsem.at[t]).start()
                pltpu.make_async_copy(rw_ref.at[:, block], wb.at[t, :, me], wsem.at[t]).start()
            else:
                there = (2 * a + core, col)
                pltpu.make_async_remote_copy(
                    x_ref.at[block], xb.at[t, me], ssem.at[0], xsem.at[t], device_id=there, device_id_type=MESH
                ).start()
                pltpu.make_async_remote_copy(
                    rw_ref.at[:, block], wb.at[t, :, me], ssem.at[1], wsem.at[t], device_id=there, device_id_type=MESH
                ).start()
        for j in range(GROUP):
            pltpu.make_async_copy(cw_ref.at[:, j * TAIL + t], cb.at[t, :, j], csem.at[t]).start()
        return carry

    lax.fori_loop(0, TAIL, send_first, 0)

    def whole(ref, sem):
        pltpu.make_async_copy(ref, ref, sem).wait()

    def row_step(t, carry):
        whole(xb.at[t], xsem.at[t])
        whole(wb.at[t], wsem.at[t])
        mix_levels(wb.at[t], xb.at[t])
        m = (me + col + t) % GROUP
        home = m == col
        for step in range(GROUP):
            i = (me + step) % GROUP

            def away():
                pltpu.make_async_remote_copy(
                    xb.at[t, i], zb.at[t, col], vsem, zsem.at[t], device_id=(2 * i + core, m), device_id_type=MESH
                ).start()

            if step == 0:
                @pl.when(home)
                def _():
                    pltpu.make_async_copy(xb.at[t, i], zb.at[t, col], zsem.at[t]).start()

                pl.when(jnp.logical_not(home))(away)
            else:
                away()
        return carry

    lax.fori_loop(0, TAIL, row_step, 0)

    def col_step(t, carry):
        whole(zb.at[t], zsem.at[t])
        whole(cb.at[t], csem.at[t])
        mix_levels(cb.at[t], zb.at[t])
        for j in range(GROUP):
            pltpu.make_async_copy(zb.at[t, j], out_ref.at[j * TAIL + t], osem).start()
        return carry

    lax.fori_loop(0, TAIL, col_step, 0)

    whole(zb, osem)
    whole(xb.at[pl.ds(0, TAIL), pl.ds(0, GROUP - 1)], ssem.at[0])
    whole(wb.at[pl.ds(0, TAIL), :, pl.ds(0, GROUP - 1)], ssem.at[1])
    whole(xb.at[pl.ds(0, TAIL), pl.ds(0, GROUP - 1)], vsem)
    whole(xb.at[0, pl.ds(0, TAIL - 1)], vsem)


def per_device(coeffs, row_weights, col_weights):
    blocks = GROUP * TAIL
    out = pl.pallas_call(
        kernel,
        out_shape=jax.ShapeDtypeStruct((blocks, R, S), jnp.float32),
        in_specs=[pl.BlockSpec(memory_space=pl.ANY)] * 3,
        out_specs=pl.BlockSpec(memory_space=pl.ANY),
        scratch_shapes=[
            pltpu.VMEM((TAIL, GROUP, R, S), jnp.float32),
            pltpu.VMEM((TAIL, LEVELS, GROUP, R, 2 * R), jnp.float32),
            pltpu.VMEM((TAIL, GROUP, R, S), jnp.float32),
            pltpu.VMEM((TAIL, LEVELS, GROUP, R, 2 * R), jnp.float32),
            pltpu.SemaphoreType.DMA((TAIL,)),
            pltpu.SemaphoreType.DMA((TAIL,)),
            pltpu.SemaphoreType.DMA((TAIL,)),
            pltpu.SemaphoreType.DMA((TAIL,)),
            pltpu.SemaphoreType.DMA,
            pltpu.SemaphoreType.DMA((2,)),
            pltpu.SemaphoreType.DMA,
        ],
        compiler_params=pltpu.CompilerParams(
            collective_id=0, has_side_effects=True, vmem_limit_bytes=48 * 1024 * 1024
        ),
        name="butterfly",
    )(
        coeffs.reshape(blocks, R, S),
        row_weights.reshape(LEVELS, blocks, R, 2 * R),
        col_weights.reshape(LEVELS, blocks, R, 2 * R),
    )
    return out.reshape(coeffs.shape)


def solution(mesh):
    return jax.shard_map(
        per_device,
        mesh=mesh,
        in_specs=(
            P("row", "col", None, None, None, None),
            P(None, "row", "col", None, None, None, None),
            P(None, "row", "col", None, None, None, None),
        ),
        out_specs=P("row", "col", None, None, None, None),
        check_vma=False,
    )
```

```python
import functools

import jax
import jax.numpy as jnp
from jax import lax
from jax.experimental import pallas as pl
from jax.experimental.pallas import tpu as pltpu
from jax.sharding import PartitionSpec as P

MESH = pl.DeviceIdType.MESH
RING = 4
PAIR = 2
GROUP = 8
TAIL = 8
R = 64
S = 512
HALF = 256
LEVELS = 3


def split(value):
    high = value.astype(jnp.bfloat16)
    low = (value - high.astype(jnp.float32)).astype(jnp.bfloat16)
    return high, low


def dot(left, right):
    return jnp.dot(left, right, preferred_element_type=jnp.float32)


def product(weights, value):
    wh, wl = weights
    xh, xl = split(value)
    return dot(wh, xh) + dot(wh, xl) + dot(wl, xh)


def mix_pair(first, second, state, a, b):
    weights = split(jnp.concatenate([first, pltpu.roll(second, R, 1)], axis=0))
    for n in range(0, S, HALF):
        cols = pl.ds(n, HALF)
        y = product(weights, jnp.concatenate([state[a, :, cols], state[b, :, cols]], axis=0))
        state[a, :, cols] = y[:R]
        state[b, :, cols] = y[R:]


def mix_level(weights, state, stride):
    for a in range(state.shape[0]):
        if not a & stride:
            b = a | stride
            mix_pair(weights(a), weights(b), state, a, b)


def mix_own(weights, state, partner, a):
    weights = split(weights)
    for n in range(0, S, HALF):
        cols = pl.ds(n, HALF)
        state[a, :, cols] = product(weights, jnp.concatenate([state[a, :, cols], partner[a, :, cols]], axis=0))


def kernel(
    x_ref, rw_ref, cw_ref, out_ref,
    xs, xp, xd, w0, wd, q, wb, x3, z4, zb, cb,
    xs_in, xp_in, xd_in, xo_in, w0_in, wd_in, wo_in, q_in, wb_in, x3_in, z4_in, zb_in, cb_in,
    sent, out_sem,
):
    row, column = lax.axis_index("row"), lax.axis_index("col")
    zl, y, core = row // GROUP, row // 2 % RING, row % 2
    x, zh = column // PAIR, column % PAIR
    near = 1 - zl
    far = 1 - zh

    def device(x, y, zh, zl):
        return (zl * GROUP + y * 2 + core, x * PAIR + zh)

    def remote(src, dst, kind, sem, there):
        pltpu.make_async_remote_copy(src, dst, sent.at[kind], sem, device_id=there, device_id_type=MESH).start()

    def local(src, dst, sem):
        pltpu.make_async_copy(src, dst, sem).start()

    def whole(ref, sem):
        pltpu.make_async_copy(ref, ref, sem).wait()

    barrier = pltpu.get_barrier_semaphore()
    partners = [device(x, y, zh, near)]
    for s in range(1, RING):
        partners += [device(x, (y + s) % RING, zh, zl), device((x + s) % RING, y, zh, zl)]
    partners += [device(x, y, far, side) for side in range(PAIR)]
    for there in partners:
        pl.semaphore_signal(barrier, 1, device_id=there, device_id_type=MESH)
    pl.semaphore_wait(barrier, len(partners))

    def send0(t):
        there = device(x, y, zh, near)
        remote(x_ref.at[:, zh, t], xp.at[t], 0, xp_in.at[t], there)
        local(x_ref.at[:, zh, t], xs.at[t], xs_in.at[t])
        local(rw_ref.at[0, :, zh, t], w0.at[t], w0_in.at[t])

    def send1(t):
        there = device(x, y, zh, near)
        for n in range(PAIR):
            mine = (x + PAIR * zl + n + t) % RING
            theirs = (x + PAIR * near + n + t) % RING
            remote(x_ref.at[theirs, far, t], xd.at[t, PAIR + n], 0, xd_in.at[t], there)
            remote(rw_ref.at[:, theirs, far, t], wd.at[t, PAIR + n], 1, wd_in.at[t], there)
            local(x_ref.at[mine, far, t], xd.at[t, n], xo_in.at[t])
            local(rw_ref.at[:, mine, far, t], wd.at[t, n], wo_in.at[t])

    def factor(t):
        local(cw_ref.at[:, :, t], cb.at[t], cb_in.at[t])
        for s in range(RING):
            yd = (y + s) % RING
            src, dst = rw_ref.at[pl.ds(1, 2), (x + yd + t) % RING, zh, t], wb.at[t, 0, y]
            if s == 0:
                local(src, dst, wb_in.at[t, 0])
            else:
                remote(src, dst, 2, wb_in.at[t, 0], device(x, yd, zh, zl))

    def across(t, side):
        return (zl + y // 2 + t + side) % 2

    def pair0(t):
        whole(xs.at[t], xs_in.at[t])
        whole(w0.at[t], w0_in.at[t])
        whole(xp.at[t], xp_in.at[t])
        for a in range(RING):
            mix_own(w0[t, a], xs.at[t], xp.at[t], a)
        for s in range(RING):
            yd = (y + s) % RING
            src, dst = xs.at[t, (x + yd + t) % RING], q.at[t, 0, y]
            if s == 0:
                local(src, dst, q_in.at[t, 0])
            else:
                remote(src, dst, 3, q_in.at[t, 0], device(x, yd, zh, zl))

    def pair1(t):
        whole(xd.at[t, pl.ds(0, PAIR)], xo_in.at[t])
        whole(xd.at[t, pl.ds(PAIR, PAIR)], xd_in.at[t])
        whole(wd.at[t, pl.ds(0, PAIR)], wo_in.at[t])
        whole(wd.at[t, pl.ds(PAIR, PAIR)], wd_in.at[t])
        for a in range(PAIR):
            mix_pair(wd[t, a, 0], wd[t, PAIR + a, 0], xd.at[t], a, PAIR + a)
        for s in range(RING):
            yd = (y + s) % RING
            there = device(x, yd, zh, zl)
            e = (yd + PAIR * (t + zh)) % RING
            src, dst = xd.at[t, e], q.at[t, 1, y]
            wsrc, wdst = wd.at[t, e, pl.ds(1, 2)], wb.at[t, 1, y]
            if s == 0:
                local(src, dst, q_in.at[t, 1])
                local(wsrc, wdst, wb_in.at[t, 1])
            else:
                remote(wsrc, wdst, 2, wb_in.at[t, 1], there)
                remote(src, dst, 3, q_in.at[t, 1], there)

    def ring_step(t, part):
        whole(wb.at[t, part], wb_in.at[t, part])
        whole(q.at[t, part], q_in.at[t, part])
        for level in range(2):
            mix_level(lambda a: wb[t, part, a, level], q.at[t, part], 2 >> level)
        shift = (y if part == 0 else PAIR * zl + y % 2) + t
        src, dst, sem = q.at[t, part], x3.at[t, part], x3_in.at[t, part]
        at_home = shift % RING == 0
        pl.when(at_home)(lambda: local(src, dst, sem))
        pl.when(jnp.logical_not(at_home))(
            lambda: remote(src, dst, 4, sem, device((x + shift) % RING, y, zh, zl))
        )

    def ring0(t):
        ring_step(t, 0)

    def ring1(t):
        ring_step(t, 1)

    def give_back(held, t, j):
        for s in range(RING):
            yi = (y + s) % RING
            src, dst = held.at[yi], zb.at[t, j]
            if s == 0:
                local(src, dst, zb_in.at[t])
            else:
                remote(src, dst, 6, zb_in.at[t], device(x, yi, zh, zl))

    def turn1(t):
        whole(x3.at[t, 1], x3_in.at[t, 1])
        remote(x3.at[t, 1], z4.at[t], 5, z4_in.at[t], device(x, y, far, across(t, zh)))

    def back0(t):
        whole(x3.at[t, 0], x3_in.at[t, 0])
        give_back(x3.at[t, 0], t, PAIR * ((x - y - t + 16) % RING) + zh)

    def back1(t):
        whole(z4.at[t], z4_in.at[t])
        give_back(z4.at[t], t, PAIR * ((x - PAIR * across(t, far) - y % 2 - t + 16) % RING) + far)

    def col(t):
        whole(cb.at[t], cb_in.at[t])
        whole(zb.at[t], zb_in.at[t])
        for level in range(LEVELS):
            mix_level(lambda a: cb[t, level, a], zb.at[t], GROUP >> level + 1)
        local(zb.at[t], out_ref.at[:, t], out_sem)

    order = (
        (send1, 2),
        (send0, 3),
        (factor, 0),
        (pair1, 3),
        (ring1, 4),
        (pair0, 4),
        (turn1, 5),
        (ring0, 5),
        (back1, 6),
        (back0, 6),
        (col, 7),
    )
    last = max(lag for _, lag in order)

    def step(n, carry):
        for work, lag in order:
            pl.when((n >= lag) & (n < TAIL + lag))(functools.partial(work, n - lag))
        return carry

    lax.fori_loop(0, TAIL + last, step, 0)

    whole(zb, out_sem)
    whole(xp, sent.at[0])
    whole(xd.at[:, pl.ds(0, PAIR)], sent.at[0])
    whole(wd.at[:, pl.ds(0, PAIR)], sent.at[1])
    whole(wb.at[:, :, pl.ds(0, RING - 1)], sent.at[2])
    whole(q.at[:, :, pl.ds(0, RING - 1)], sent.at[3])
    whole(x3.at[pl.ds(0, TAIL - TAIL // RING)], sent.at[4])
    whole(z4, sent.at[5])
    whole(zb.at[:, pl.ds(0, GROUP - PAIR)], sent.at[6])


def per_device(coeffs, row_weights, col_weights):
    block, factor = (R, S), (R, 2 * R)
    buffers = [
        (TAIL, RING) + block,
        (TAIL, RING) + block,
        (TAIL, RING) + block,
        (TAIL, RING) + factor,
        (TAIL, RING, LEVELS) + factor,
        (TAIL, PAIR, RING) + block,
        (TAIL, PAIR, RING, LEVELS - 1) + factor,
        (TAIL, PAIR, RING) + block,
        (TAIL, RING) + block,
        (TAIL, GROUP) + block,
        (TAIL, LEVELS, GROUP) + factor,
    ]
    out = pl.pallas_call(
        kernel,
        out_shape=jax.ShapeDtypeStruct((GROUP, TAIL) + block, jnp.float32),
        in_specs=[pl.BlockSpec(memory_space=pl.ANY)] * 3,
        out_specs=pl.BlockSpec(memory_space=pl.ANY),
        scratch_shapes=[pltpu.VMEM(shape, jnp.float32) for shape in buffers]
        + [pltpu.SemaphoreType.DMA((TAIL,))] * 7
        + [pltpu.SemaphoreType.DMA((TAIL, PAIR))] * 3
        + [pltpu.SemaphoreType.DMA((TAIL,))] * 3
        + [pltpu.SemaphoreType.DMA((7,)), pltpu.SemaphoreType.DMA],
        compiler_params=pltpu.CompilerParams(
            collective_id=0, has_side_effects=True, vmem_limit_bytes=60 * 1024 * 1024
        ),
        name="butterfly",
    )(
        coeffs.reshape((RING, PAIR, TAIL) + block),
        row_weights.reshape((LEVELS, RING, PAIR, TAIL) + factor),
        col_weights.reshape((LEVELS, GROUP, TAIL) + factor),
    )
    return out.reshape(coeffs.shape)


def solution(mesh):
    return jax.shard_map(
        per_device,
        mesh=mesh,
        in_specs=(
            P("row", "col", None, None, None, None),
            P(None, "row", "col", None, None, None, None),
            P(None, "row", "col", None, None, None, None),
        ),
        out_specs=P("row", "col", None, None, None, None),
        check_vma=False,
    )
```

```python
import functools

import jax
import jax.numpy as jnp
from jax import lax
from jax.experimental import pallas as pl
from jax.experimental.pallas import tpu as pltpu
from jax.sharding import PartitionSpec as P

MESH = pl.DeviceIdType.MESH
RING = 4
PAIR = 2
GROUP = 8
TAIL = 8
R = 64
S = 512
PIECES = 2
WIDTH = S // PIECES
STEPS = TAIL * PIECES
LEVELS = 3


def split(value):
    high = value.astype(jnp.bfloat16)
    low = (value - high.astype(jnp.float32)).astype(jnp.bfloat16)
    return high, low


def dot(left, right):
    return jnp.dot(left, right, preferred_element_type=jnp.float32)


def product(weights, value):
    wh, wl = weights
    xh, xl = split(value)
    return dot(wh, xh) + dot(wh, xl) + dot(wl, xh)


def mix_pair(first, second, state, a, b):
    weights = split(jnp.concatenate([first, pltpu.roll(second, R, 1)], axis=0))
    y = product(weights, jnp.concatenate([state[a], state[b]], axis=0))
    state[a] = y[:R]
    state[b] = y[R:]


def mix_level(weights, state, stride):
    for a in range(state.shape[0]):
        if not a & stride:
            b = a | stride
            mix_pair(weights(a), weights(b), state, a, b)


def mix_own(weights, state, partner, a):
    state[a] = product(split(weights), jnp.concatenate([state[a], partner[a]], axis=0))


def kernel(
    x_ref, rw_ref, cw_ref, zb,
    xs, xp, xd, w0, wd, q, wb, x3, z4, cb,
    xs_in, xp_in, xd_in, xo_in, w0_in, wd_in, wo_in, q_in, wb_in, x3_in, z4_in, zb_in, cb_in,
    sent,
):
    row, column = lax.axis_index("row"), lax.axis_index("col")
    zl, y, core = row // GROUP, row // 2 % RING, row % 2
    x, zh = column // PAIR, column % PAIR
    near = 1 - zl
    far = 1 - zh

    def device(x, y, zh, zl):
        return (zl * GROUP + y * 2 + core, x * PAIR + zh)

    def remote(src, dst, kind, sem, there):
        pltpu.make_async_remote_copy(src, dst, sent.at[kind], sem, device_id=there, device_id_type=MESH).start()

    def local(src, dst, sem):
        pltpu.make_async_copy(src, dst, sem).start()

    def whole(ref, sem):
        pltpu.make_async_copy(ref, ref, sem).wait()

    barrier = pltpu.get_barrier_semaphore()
    partners = [device(x, y, zh, near)]
    for s in range(1, RING):
        partners += [device(x, (y + s) % RING, zh, zl), device((x + s) % RING, y, zh, zl)]
    partners += [device(x, y, far, side) for side in range(PAIR)]
    for there in partners:
        pl.semaphore_signal(barrier, 1, device_id=there, device_id_type=MESH)
    pl.semaphore_wait(barrier, len(partners))

    def piece(n):
        return n // PIECES, pl.ds(pl.multiple_of(n % PIECES * WIDTH, WIDTH), WIDTH)

    def once(n, work):
        pl.when(n % PIECES == 0)(work)

    def send0(n):
        t, cols = piece(n)
        remote(x_ref.at[:, zh, t, :, cols], xp.at[n], 0, xp_in.at[n], device(x, y, zh, near))
        local(x_ref.at[:, zh, t, :, cols], xs.at[n], xs_in.at[n])
        once(n, lambda: local(rw_ref.at[0, :, zh, t], w0.at[t], w0_in.at[t]))

    def send1(n):
        t, cols = piece(n)
        there = device(x, y, zh, near)
        for a in range(PAIR):
            mine = (x + PAIR * zl + a + t) % RING
            theirs = (x + PAIR * near + a + t) % RING

            @functools.partial(once, n)
            def _():
                remote(rw_ref.at[:, theirs, far, t], wd.at[t, PAIR + a], 1, wd_in.at[t], there)
                local(rw_ref.at[:, mine, far, t], wd.at[t, a], wo_in.at[t])

            remote(x_ref.at[theirs, far, t, :, cols], xd.at[n, PAIR + a], 0, xd_in.at[n], there)
            local(x_ref.at[mine, far, t, :, cols], xd.at[n, a], xo_in.at[n])

    def send_factor(src, dst, sem, s, yd):
        if s == 0:
            local(src, dst, sem)
        else:
            remote(src, dst, 2, sem, device(x, yd, zh, zl))

    def factor(n):
        t, _ = piece(n)

        @functools.partial(once, n)
        def _():
            local(cw_ref.at[:, :, t], cb.at[t], cb_in.at[t])
            for s in range(RING):
                yd = (y + s) % RING
                send_factor(rw_ref.at[pl.ds(1, 2), (x + yd + t) % RING, zh, t], wb.at[t, 0, y], wb_in.at[t, 0], s, yd)

    def across(t, side):
        return (zl + y // 2 + t + side) % 2

    def spread(src, dst, sem, s, yd):
        if s == 0:
            local(src, dst, sem)
        else:
            remote(src, dst, 3, sem, device(x, yd, zh, zl))

    def pair0(n):
        t, _ = piece(n)
        once(n, lambda: whole(w0.at[t], w0_in.at[t]))
        whole(xs.at[n], xs_in.at[n])
        whole(xp.at[n], xp_in.at[n])
        for a in range(RING):
            mix_own(w0[t, a], xs.at[n], xp.at[n], a)
        for s in range(RING):
            yd = (y + s) % RING
            spread(xs.at[n, (x + yd + t) % RING], q.at[n, 0, y], q_in.at[n, 0], s, yd)

    def pair1(n):
        t, _ = piece(n)

        @functools.partial(once, n)
        def _():
            whole(wd.at[t, pl.ds(0, PAIR)], wo_in.at[t])
            whole(wd.at[t, pl.ds(PAIR, PAIR)], wd_in.at[t])
            for s in range(RING):
                yd = (y + s) % RING
                e = (yd + PAIR * (t + zh)) % RING
                send_factor(wd.at[t, e, pl.ds(1, 2)], wb.at[t, 1, y], wb_in.at[t, 1], s, yd)

        whole(xd.at[n, pl.ds(0, PAIR)], xo_in.at[n])
        whole(xd.at[n, pl.ds(PAIR, PAIR)], xd_in.at[n])
        for a in range(PAIR):
            mix_pair(wd[t, a, 0], wd[t, PAIR + a, 0], xd.at[n], a, PAIR + a)
        for s in range(RING):
            yd = (y + s) % RING
            spread(xd.at[n, (yd + PAIR * (t + zh)) % RING], q.at[n, 1, y], q_in.at[n, 1], s, yd)

    def ring_step(n, part):
        t, _ = piece(n)
        once(n, lambda: whole(wb.at[t, part], wb_in.at[t, part]))
        whole(q.at[n, part], q_in.at[n, part])
        for level in range(2):
            mix_level(lambda a: wb[t, part, a, level], q.at[n, part], 2 >> level)
        shift = (y if part == 0 else PAIR * zl + y % 2) + t
        src, dst, sem = q.at[n, part], x3.at[n, part], x3_in.at[n, part]
        at_home = shift % RING == 0
        pl.when(at_home)(lambda: local(src, dst, sem))
        pl.when(jnp.logical_not(at_home))(
            lambda: remote(src, dst, 4, sem, device((x + shift) % RING, y, zh, zl))
        )

    def ring0(n):
        ring_step(n, 0)

    def ring1(n):
        ring_step(n, 1)

    def give_back(held, n, j):
        t, cols = piece(n)
        for s in range(RING):
            yi = (y + s) % RING
            src, dst = held.at[yi], zb.at[j, t, :, cols]
            if s == 0:
                local(src, dst, zb_in.at[n])
            else:
                remote(src, dst, 6, zb_in.at[n], device(x, yi, zh, zl))

    def turn1(n):
        t, _ = piece(n)
        whole(x3.at[n, 1], x3_in.at[n, 1])
        remote(x3.at[n, 1], z4.at[n], 5, z4_in.at[n], device(x, y, far, across(t, zh)))

    def back0(n):
        t, _ = piece(n)
        whole(x3.at[n, 0], x3_in.at[n, 0])
        give_back(x3.at[n, 0], n, PAIR * ((x - y - t + 16) % RING) + zh)

    def back1(n):
        t, _ = piece(n)
        whole(z4.at[n], z4_in.at[n])
        give_back(z4.at[n], n, PAIR * ((x - PAIR * across(t, far) - y % 2 - t + 16) % RING) + far)

    def col(n):
        t, cols = piece(n)
        once(n, lambda: whole(cb.at[t], cb_in.at[t]))
        state = zb.at[:, t, :, cols]
        whole(state, zb_in.at[n])
        for level in range(LEVELS):
            mix_level(lambda a: cb[t, level, a], state, GROUP >> level + 1)

    order = (
        (send1, 4),
        (factor, 0),
        (pair1, 5),
        (ring1, 6),
        (send0, 5),
        (turn1, 6),
        (pair0, 6),
        (ring0, 7),
        (back1, 7),
        (back0, 8),
        (col, 9),
    )
    last = max(lag for _, lag in order)

    def step(n, carry):
        for work, lag in order:
            pl.when((n >= lag) & (n < STEPS + lag))(functools.partial(work, n - lag))
        return carry

    lax.fori_loop(0, STEPS + last, step, 0)

    whole(xp, sent.at[0])
    whole(xd.at[:, pl.ds(0, PAIR)], sent.at[0])
    whole(wd.at[:, pl.ds(0, PAIR)], sent.at[1])
    whole(wb.at[:, :, pl.ds(0, RING - 1)], sent.at[2])
    whole(q.at[:, :, pl.ds(0, RING - 1)], sent.at[3])
    whole(x3.at[pl.ds(0, STEPS - STEPS // RING)], sent.at[4])
    whole(z4, sent.at[5])
    whole(zb.at[pl.ds(0, GROUP - PAIR)], sent.at[6])


def per_device(coeffs, row_weights, col_weights):
    block, factor, part = (R, S), (R, 2 * R), (R, WIDTH)
    buffers = [
        (STEPS, RING) + part,
        (STEPS, RING) + part,
        (STEPS, RING) + part,
        (TAIL, RING) + factor,
        (TAIL, RING, LEVELS) + factor,
        (STEPS, PAIR, RING) + part,
        (TAIL, PAIR, RING, LEVELS - 1) + factor,
        (STEPS, PAIR, RING) + part,
        (STEPS, RING) + part,
        (TAIL, LEVELS, GROUP) + factor,
    ]
    out = pl.pallas_call(
        kernel,
        out_shape=pltpu.VMEM((GROUP, TAIL) + block, jnp.float32),
        in_specs=[pl.BlockSpec(memory_space=pl.ANY)] * 3,
        out_specs=pl.BlockSpec(memory_space=pltpu.VMEM),
        scratch_shapes=[pltpu.VMEM(shape, jnp.float32) for shape in buffers]
        + [pltpu.SemaphoreType.DMA((STEPS,))] * 4
        + [pltpu.SemaphoreType.DMA((TAIL,))] * 3
        + [pltpu.SemaphoreType.DMA((STEPS, PAIR))]
        + [pltpu.SemaphoreType.DMA((TAIL, PAIR))]
        + [pltpu.SemaphoreType.DMA((STEPS, PAIR))]
        + [pltpu.SemaphoreType.DMA((STEPS,))] * 2
        + [pltpu.SemaphoreType.DMA((TAIL,))]
        + [pltpu.SemaphoreType.DMA((7,))],
        compiler_params=pltpu.CompilerParams(
            collective_id=0, has_side_effects=True, vmem_limit_bytes=50 * 1024 * 1024
        ),
        name="butterfly",
    )(
        coeffs.reshape((RING, PAIR, TAIL) + block),
        row_weights.reshape((LEVELS, RING, PAIR, TAIL) + factor),
        col_weights.reshape((LEVELS, GROUP, TAIL) + factor),
    )
    return out.reshape(coeffs.shape)


def solution(mesh):
    return jax.shard_map(
        per_device,
        mesh=mesh,
        in_specs=(
            P("row", "col", None, None, None, None),
            P(None, "row", "col", None, None, None, None),
            P(None, "row", "col", None, None, None, None),
        ),
        out_specs=P("row", "col", None, None, None, None),
        check_vma=False,
    )
```

```python
import functools

import jax
import jax.numpy as jnp
from jax import lax
from jax.experimental import pallas as pl
from jax.experimental.pallas import tpu as pltpu
from jax.sharding import PartitionSpec as P

MESH = pl.DeviceIdType.MESH
RING = 4
PAIR = 2
GROUP = 8
TAIL = 8
R = 64
S = 512
PIECES = 2
WIDTH = S // PIECES
STEPS = TAIL * PIECES
LEVELS = 3


def split(value):
    high = value.astype(jnp.bfloat16)
    low = (value - high.astype(jnp.float32)).astype(jnp.bfloat16)
    return high, low


def dot(left, right):
    return jnp.dot(left, right, preferred_element_type=jnp.float32)


def product(weights, value):
    wh, wl = weights
    xh, xl = split(value)
    return dot(wh, xh) + dot(wh, xl) + dot(wl, xh)


def mix_pair(first, second, state, a, b):
    weights = split(jnp.concatenate([first, pltpu.roll(second, R, 1)], axis=0))
    y = product(weights, jnp.concatenate([state[a], state[b]], axis=0))
    state[a] = y[:R]
    state[b] = y[R:]


def mix_level(weights, state, stride):
    for a in range(state.shape[0]):
        if not a & stride:
            b = a | stride
            mix_pair(weights(a), weights(b), state, a, b)


def mix_own(weights, state, partner, a):
    state[a] = product(split(weights), jnp.concatenate([state[a], partner[a]], axis=0))


def kernel(
    x_ref, rw_ref, cw_ref, zb,
    xs, xp, xd, w0, wd, q, wb, x3, z4, cb,
    xs_in, xp_in, xd_in, xo_in, w0_in, wd_in, wo_in, q_in, wb_in, x3_in, z4_in, zb_in, cb_in,
    sent,
):
    row, column = lax.axis_index("row"), lax.axis_index("col")
    zl, y, core = row // GROUP, row // 2 % RING, row % 2
    x, zh = column // PAIR, column % PAIR
    near = 1 - zl
    far = 1 - zh

    def device(x, y, zh, zl):
        return (zl * GROUP + y * 2 + core, x * PAIR + zh)

    def remote(src, dst, kind, sem, there):
        pltpu.make_async_remote_copy(src, dst, sent.at[kind], sem, device_id=there, device_id_type=MESH).start()

    def local(src, dst, sem):
        pltpu.make_async_copy(src, dst, sem).start()

    def whole(ref, sem):
        pltpu.make_async_copy(ref, ref, sem).wait()

    barrier = pltpu.get_barrier_semaphore()
    partners = [device(x, y, zh, near)]
    for s in range(1, RING):
        partners += [device(x, (y + s) % RING, zh, zl), device((x + s) % RING, y, zh, zl)]
    partners += [device(x, y, far, side) for side in range(PAIR)]
    for there in partners:
        pl.semaphore_signal(barrier, 1, device_id=there, device_id_type=MESH)
    pl.semaphore_wait(barrier, len(partners))

    def piece(n):
        return n // PIECES, pl.ds(pl.multiple_of(n % PIECES * WIDTH, WIDTH), WIDTH)

    def once(n, work):
        pl.when(n % PIECES == 0)(work)

    def send0(n):
        t, cols = piece(n)
        remote(x_ref.at[:, zh, t, :, cols], xp.at[n], 0, xp_in.at[n], device(x, y, zh, near))
        local(x_ref.at[:, zh, t, :, cols], xs.at[n], xs_in.at[n])
        once(n, lambda: local(rw_ref.at[0, :, zh, t], w0.at[t], w0_in.at[t]))

    def send1(n):
        t, cols = piece(n)
        there = device(x, y, zh, near)
        for a in range(PAIR):
            mine = (x + PAIR * zl + a + t) % RING
            theirs = (x + PAIR * near + a + t) % RING

            @functools.partial(once, n)
            def _():
                remote(rw_ref.at[:, theirs, far, t], wd.at[t, PAIR + a], 1, wd_in.at[t], there)
                local(rw_ref.at[:, mine, far, t], wd.at[t, a], wo_in.at[t])

            remote(x_ref.at[theirs, far, t, :, cols], xd.at[n, PAIR + a], 0, xd_in.at[n], there)
            local(x_ref.at[mine, far, t, :, cols], xd.at[n, a], xo_in.at[n])

    def send_factor(src, dst, sem, s, yd):
        if s == 0:
            local(src, dst, sem)
        else:
            remote(src, dst, 2, sem, device(x, yd, zh, zl))

    def factor(n):
        t, _ = piece(n)

        @functools.partial(once, n)
        def _():
            local(cw_ref.at[:, :, t], cb.at[t], cb_in.at[t])
            for s in range(RING):
                yd = (y + s) % RING
                send_factor(rw_ref.at[pl.ds(1, 2), (x + yd + t) % RING, zh, t], wb.at[t, 0, y], wb_in.at[t, 0], s, yd)

    def across(t, side):
        return (zl + y // 2 + t + side) % 2

    def spread(src, dst, sem, s, yd):
        if s == 0:
            local(src, dst, sem)
        else:
            remote(src, dst, 3, sem, device(x, yd, zh, zl))

    def pair0(n):
        t, _ = piece(n)
        once(n, lambda: whole(w0.at[t], w0_in.at[t]))
        whole(xs.at[n], xs_in.at[n])
        whole(xp.at[n], xp_in.at[n])
        for a in range(RING):
            mix_own(w0[t, a], xs.at[n], xp.at[n], a)
        for s in range(RING):
            yd = (y + s) % RING
            spread(xs.at[n, (x + yd + t) % RING], q.at[n, 0, y], q_in.at[n, 0], s, yd)

    def pair1(n):
        t, _ = piece(n)

        @functools.partial(once, n)
        def _():
            whole(wd.at[t, pl.ds(0, PAIR)], wo_in.at[t])
            whole(wd.at[t, pl.ds(PAIR, PAIR)], wd_in.at[t])
            for s in range(RING):
                yd = (y + s) % RING
                e = (yd + PAIR * (t + zh)) % RING
                send_factor(wd.at[t, e, pl.ds(1, 2)], wb.at[t, 1, y], wb_in.at[t, 1], s, yd)

        whole(xd.at[n, pl.ds(0, PAIR)], xo_in.at[n])
        whole(xd.at[n, pl.ds(PAIR, PAIR)], xd_in.at[n])
        for a in range(PAIR):
            mix_pair(wd[t, a, 0], wd[t, PAIR + a, 0], xd.at[n], a, PAIR + a)
        for s in range(RING):
            yd = (y + s) % RING
            spread(xd.at[n, (yd + PAIR * (t + zh)) % RING], q.at[n, 1, y], q_in.at[n, 1], s, yd)

    def ring_step(n, part):
        t, _ = piece(n)
        once(n, lambda: whole(wb.at[t, part], wb_in.at[t, part]))
        whole(q.at[n, part], q_in.at[n, part])
        for level in range(2):
            mix_level(lambda a: wb[t, part, a, level], q.at[n, part], 2 >> level)
        shift = (y if part == 0 else PAIR * zl + y % 2) + t
        src, dst, sem = q.at[n, part], x3.at[n, part], x3_in.at[n, part]
        at_home = shift % RING == 0
        pl.when(at_home)(lambda: local(src, dst, sem))
        pl.when(jnp.logical_not(at_home))(
            lambda: remote(src, dst, 4, sem, device((x + shift) % RING, y, zh, zl))
        )

    def ring0(n):
        ring_step(n, 0)

    def ring1(n):
        ring_step(n, 1)

    def give_back(held, n, j):
        t, cols = piece(n)
        for s in range(RING):
            yi = (y + s) % RING
            src, dst = held.at[yi], zb.at[j, t, :, cols]
            if s == 0:
                local(src, dst, zb_in.at[n])
            else:
                remote(src, dst, 6, zb_in.at[n], device(x, yi, zh, zl))

    def turn1(n):
        t, _ = piece(n)
        whole(x3.at[n, 1], x3_in.at[n, 1])
        remote(x3.at[n, 1], z4.at[n], 5, z4_in.at[n], device(x, y, far, across(t, zh)))

    def back0(n):
        t, _ = piece(n)
        whole(x3.at[n, 0], x3_in.at[n, 0])
        give_back(x3.at[n, 0], n, PAIR * ((x - y - t + 16) % RING) + zh)

    def back1(n):
        t, _ = piece(n)
        whole(z4.at[n], z4_in.at[n])
        give_back(z4.at[n], n, PAIR * ((x - PAIR * across(t, far) - y % 2 - t + 16) % RING) + far)

    def col(n):
        t, cols = piece(n)
        once(n, lambda: whole(cb.at[t], cb_in.at[t]))
        state = zb.at[:, t, :, cols]
        whole(state, zb_in.at[n])
        for level in range(LEVELS):
            mix_level(lambda a: cb[t, level, a], state, GROUP >> level + 1)

    order = (
        (col, 12),
        (send1, 4),
        (turn1, 8),
        (factor, 0),
        (back1, 10),
        (back0, 9),
        (ring0, 8),
        (ring1, 6),
        (pair1, 5),
        (pair0, 7),
        (send0, 6),
    )
    last = max(lag for _, lag in order)

    def step(n, carry):
        for work, lag in order:
            pl.when((n >= lag) & (n < STEPS + lag))(functools.partial(work, n - lag))
        return carry

    lax.fori_loop(0, STEPS + last, step, 0)

    whole(xp, sent.at[0])
    whole(xd.at[:, pl.ds(0, PAIR)], sent.at[0])
    whole(wd.at[:, pl.ds(0, PAIR)], sent.at[1])
    whole(wb.at[:, :, pl.ds(0, RING - 1)], sent.at[2])
    whole(q.at[:, :, pl.ds(0, RING - 1)], sent.at[3])
    whole(x3.at[pl.ds(0, STEPS - STEPS // RING)], sent.at[4])
    whole(z4, sent.at[5])
    whole(zb.at[pl.ds(0, GROUP - PAIR)], sent.at[6])


def per_device(coeffs, row_weights, col_weights):
    block, factor, part = (R, S), (R, 2 * R), (R, WIDTH)
    buffers = [
        (STEPS, RING) + part,
        (STEPS, RING) + part,
        (STEPS, RING) + part,
        (TAIL, RING) + factor,
        (TAIL, RING, LEVELS) + factor,
        (STEPS, PAIR, RING) + part,
        (TAIL, PAIR, RING, LEVELS - 1) + factor,
        (STEPS, PAIR, RING) + part,
        (STEPS, RING) + part,
        (TAIL, LEVELS, GROUP) + factor,
    ]
    out = pl.pallas_call(
        kernel,
        out_shape=pltpu.VMEM((GROUP, TAIL) + block, jnp.float32),
        in_specs=[pl.BlockSpec(memory_space=pl.ANY)] * 3,
        out_specs=pl.BlockSpec(memory_space=pltpu.VMEM),
        scratch_shapes=[pltpu.VMEM(shape, jnp.float32) for shape in buffers]
        + [pltpu.SemaphoreType.DMA((STEPS,))] * 4
        + [pltpu.SemaphoreType.DMA((TAIL,))] * 3
        + [pltpu.SemaphoreType.DMA((STEPS, PAIR))]
        + [pltpu.SemaphoreType.DMA((TAIL, PAIR))]
        + [pltpu.SemaphoreType.DMA((STEPS, PAIR))]
        + [pltpu.SemaphoreType.DMA((STEPS,))] * 2
        + [pltpu.SemaphoreType.DMA((TAIL,))]
        + [pltpu.SemaphoreType.DMA((7,))],
        compiler_params=pltpu.CompilerParams(
            collective_id=0, has_side_effects=True, vmem_limit_bytes=50 * 1024 * 1024
        ),
        name="butterfly",
    )(
        coeffs.reshape((RING, PAIR, TAIL) + block),
        row_weights.reshape((LEVELS, RING, PAIR, TAIL) + factor),
        col_weights.reshape((LEVELS, GROUP, TAIL) + factor),
    )
    return out.reshape(coeffs.shape)


def solution(mesh):
    return jax.shard_map(
        per_device,
        mesh=mesh,
        in_specs=(
            P("row", "col", None, None, None, None),
            P(None, "row", "col", None, None, None, None),
            P(None, "row", "col", None, None, None, None),
        ),
        out_specs=P("row", "col", None, None, None, None),
        check_vma=False,
    )
```

```python
import functools

import jax
import jax.numpy as jnp
from jax import lax
from jax.experimental import pallas as pl
from jax.experimental.pallas import tpu as pltpu
from jax.sharding import PartitionSpec as P

MESH = pl.DeviceIdType.MESH
RING = 4
PAIR = 2
GROUP = 8
TAIL = 8
R = 64
S = 512
PIECES = 2
WIDTH = S // PIECES
STEPS = TAIL * PIECES
LEVELS = 3


def split(value):
    high = value.astype(jnp.bfloat16)
    low = (value - high.astype(jnp.float32)).astype(jnp.bfloat16)
    return high, low


def product(weights, value):
    wh, wl = weights
    xh, xl = split(value)
    return jnp.dot(
        jnp.concatenate([wh, wl, wh], axis=1),
        jnp.concatenate([xh, xh, xl], axis=0),
        preferred_element_type=jnp.float32,
    )


def mix_pair(first, second, state, a, b):
    weights = split(jnp.concatenate([first, pltpu.roll(second, R, 1)], axis=0))
    y = product(weights, jnp.concatenate([state[a], state[b]], axis=0))
    state[a] = y[:R]
    state[b] = y[R:]


def mix_level(weights, state, stride):
    for a in range(state.shape[0]):
        if not a & stride:
            b = a | stride
            mix_pair(weights(a), weights(b), state, a, b)


def mix_own(weights, state, partner, a):
    state[a] = product(split(weights), jnp.concatenate([state[a], partner[a]], axis=0))


def kernel(
    x_ref, rw_ref, cw_ref, zb,
    xs, xp, xd, w0, wd, q, wb, x3, z4, cb,
    xs_in, xp_in, xd_in, xo_in, w0_in, wd_in, wo_in, q_in, wb_in, x3_in, z4_in, zb_in, cb_in,
    sent,
):
    row, column = lax.axis_index("row"), lax.axis_index("col")
    zl, y, core = row // GROUP, row // 2 % RING, row % 2
    x, zh = column // PAIR, column % PAIR
    near = 1 - zl
    far = 1 - zh

    def device(x, y, zh, zl):
        return (zl * GROUP + y * 2 + core, x * PAIR + zh)

    def remote(src, dst, kind, sem, there):
        pltpu.make_async_remote_copy(src, dst, sent.at[kind], sem, device_id=there, device_id_type=MESH).start()

    def local(src, dst, sem):
        pltpu.make_async_copy(src, dst, sem).start()

    def whole(ref, sem):
        pltpu.make_async_copy(ref, ref, sem).wait()

    barrier = pltpu.get_barrier_semaphore()
    partners = [device(x, y, zh, near)]
    for s in range(1, RING):
        partners += [device(x, (y + s) % RING, zh, zl), device((x + s) % RING, y, zh, zl)]
    partners += [device(x, y, far, side) for side in range(PAIR)]
    for there in partners:
        pl.semaphore_signal(barrier, 1, device_id=there, device_id_type=MESH)
    pl.semaphore_wait(barrier, len(partners))

    def place(n):
        return n // PIECES, n % PIECES

    def piece(n):
        t, part = place(n)
        return t, pl.ds(pl.multiple_of(part * WIDTH, WIDTH), WIDTH)

    def once(n, work):
        pl.when(place(n)[1] == 0)(work)

    def send0(n):
        t, cols = piece(n)
        remote(x_ref.at[:, zh, t, :, cols], xp.at[n], 0, xp_in.at[n], device(x, y, zh, near))
        local(x_ref.at[:, zh, t, :, cols], xs.at[n], xs_in.at[n])
        once(n, lambda: local(rw_ref.at[0, :, zh, t], w0.at[t], w0_in.at[t]))

    def send1(n):
        t, cols = piece(n)
        there = device(x, y, zh, near)
        for a in range(PAIR):
            mine = (x + PAIR * zl + a + t) % RING
            theirs = (x + PAIR * near + a + t) % RING

            @functools.partial(once, n)
            def _():
                remote(rw_ref.at[:, theirs, far, t], wd.at[t, PAIR + a], 1, wd_in.at[t], there)
                local(rw_ref.at[:, mine, far, t], wd.at[t, a], wo_in.at[t])

            remote(x_ref.at[theirs, far, t, :, cols], xd.at[n, PAIR + a], 0, xd_in.at[n], there)
            local(x_ref.at[mine, far, t, :, cols], xd.at[n, a], xo_in.at[n])

    def send_factor(src, dst, sem, s, yd):
        if s == 0:
            local(src, dst, sem)
        else:
            remote(src, dst, 2, sem, device(x, yd, zh, zl))

    def factor(n):
        t, _ = piece(n)

        @functools.partial(once, n)
        def _():
            local(cw_ref.at[:, :, t], cb.at[t], cb_in.at[t])
            for s in range(RING):
                yd = (y + s) % RING
                send_factor(rw_ref.at[pl.ds(1, 2), (x + yd + t) % RING, zh, t], wb.at[t, 0, y], wb_in.at[t, 0], s, yd)

    def across(t, side):
        return (zl + y // 2 + t + side) % 2

    def spread(src, dst, sem, s, yd):
        if s == 0:
            local(src, dst, sem)
        else:
            remote(src, dst, 3, sem, device(x, yd, zh, zl))

    def pair0(n):
        t, _ = piece(n)
        once(n, lambda: whole(w0.at[t], w0_in.at[t]))
        whole(xs.at[n], xs_in.at[n])
        whole(xp.at[n], xp_in.at[n])
        for a in range(RING):
            mix_own(w0[t, a], xs.at[n], xp.at[n], a)
        for s in range(RING):
            yd = (y + s) % RING
            spread(xs.at[n, (x + yd + t) % RING], q.at[n, 0, y], q_in.at[n, 0], s, yd)

    def pair1(n):
        t, _ = piece(n)

        @functools.partial(once, n)
        def _():
            whole(wd.at[t, pl.ds(0, PAIR)], wo_in.at[t])
            whole(wd.at[t, pl.ds(PAIR, PAIR)], wd_in.at[t])
            for s in range(RING):
                yd = (y + s) % RING
                e = (yd + PAIR * (t + zh)) % RING
                send_factor(wd.at[t, e, pl.ds(1, 2)], wb.at[t, 1, y], wb_in.at[t, 1], s, yd)

        whole(xd.at[n, pl.ds(0, PAIR)], xo_in.at[n])
        whole(xd.at[n, pl.ds(PAIR, PAIR)], xd_in.at[n])
        for a in range(PAIR):
            mix_pair(wd[t, a, 0], wd[t, PAIR + a, 0], xd.at[n], a, PAIR + a)
        for s in range(RING):
            yd = (y + s) % RING
            spread(xd.at[n, (yd + PAIR * (t + zh)) % RING], q.at[n, 1, y], q_in.at[n, 1], s, yd)

    def ring_step(n, part):
        t, _ = piece(n)
        once(n, lambda: whole(wb.at[t, part], wb_in.at[t, part]))
        whole(q.at[n, part], q_in.at[n, part])
        for level in range(2):
            mix_level(lambda a: wb[t, part, a, level], q.at[n, part], 2 >> level)
        shift = (y if part == 0 else PAIR * zl + y % 2) + t
        src, dst, sem = q.at[n, part], x3.at[n, part], x3_in.at[n, part]
        at_home = shift % RING == 0
        pl.when(at_home)(lambda: local(src, dst, sem))
        pl.when(jnp.logical_not(at_home))(
            lambda: remote(src, dst, 4, sem, device((x + shift) % RING, y, zh, zl))
        )

    def ring0(n):
        ring_step(n, 0)

    def ring1(n):
        ring_step(n, 1)

    def give_back(held, n, j):
        t, cols = piece(n)
        for s in range(RING):
            yi = (y + s) % RING
            src, dst = held.at[yi], zb.at[j, t, :, cols]
            if s == 0:
                local(src, dst, zb_in.at[n])
            else:
                remote(src, dst, 6, zb_in.at[n], device(x, yi, zh, zl))

    def turn1(n):
        t, _ = piece(n)
        whole(x3.at[n, 1], x3_in.at[n, 1])
        remote(x3.at[n, 1], z4.at[n], 5, z4_in.at[n], device(x, y, far, across(t, zh)))

    def back0(n):
        t, _ = piece(n)
        whole(x3.at[n, 0], x3_in.at[n, 0])
        give_back(x3.at[n, 0], n, PAIR * ((x - y - t + 16) % RING) + zh)

    def back1(n):
        t, _ = piece(n)
        whole(z4.at[n], z4_in.at[n])
        give_back(z4.at[n], n, PAIR * ((x - PAIR * across(t, far) - y % 2 - t + 16) % RING) + far)

    def col(n):
        t, cols = piece(n)
        once(n, lambda: whole(cb.at[t], cb_in.at[t]))
        state = zb.at[:, t, :, cols]
        whole(state, zb_in.at[n])
        for level in range(LEVELS):
            mix_level(lambda a: cb[t, level, a], state, GROUP >> level + 1)

    order = (
        (col, 12),
        (send1, 4),
        (back1, 10),
        (turn1, 8),
        (factor, 0),
        (back0, 9),
        (ring0, 8),
        (ring1, 6),
        (pair1, 5),
        (send0, 6),
        (pair0, 7),
    )
    last = max(lag for _, lag in order)

    def step(n, carry):
        for work, lag in order:
            pl.when((n >= lag) & (n < STEPS + lag))(functools.partial(work, n - lag))
        return carry

    lax.fori_loop(0, STEPS + last, step, 0)

    whole(xp, sent.at[0])
    whole(xd.at[:, pl.ds(0, PAIR)], sent.at[0])
    whole(wd.at[:, pl.ds(0, PAIR)], sent.at[1])
    whole(wb.at[:, :, pl.ds(0, RING - 1)], sent.at[2])
    whole(q.at[:, :, pl.ds(0, RING - 1)], sent.at[3])
    whole(x3.at[pl.ds(0, STEPS - STEPS // RING)], sent.at[4])
    whole(z4, sent.at[5])
    whole(zb.at[pl.ds(0, GROUP - PAIR)], sent.at[6])


def per_device(coeffs, row_weights, col_weights):
    block, factor, part = (R, S), (R, 2 * R), (R, WIDTH)
    buffers = [
        (STEPS, RING) + part,
        (STEPS, RING) + part,
        (STEPS, RING) + part,
        (TAIL, RING) + factor,
        (TAIL, RING, LEVELS) + factor,
        (STEPS, PAIR, RING) + part,
        (TAIL, PAIR, RING, LEVELS - 1) + factor,
        (STEPS, PAIR, RING) + part,
        (STEPS, RING) + part,
        (TAIL, LEVELS, GROUP) + factor,
    ]
    out = pl.pallas_call(
        kernel,
        out_shape=pltpu.VMEM((GROUP, TAIL) + block, jnp.float32),
        in_specs=[pl.BlockSpec(memory_space=pl.ANY)] * 3,
        out_specs=pl.BlockSpec(memory_space=pltpu.VMEM),
        scratch_shapes=[pltpu.VMEM(shape, jnp.float32) for shape in buffers]
        + [pltpu.SemaphoreType.DMA((STEPS,))] * 4
        + [pltpu.SemaphoreType.DMA((TAIL,))] * 3
        + [pltpu.SemaphoreType.DMA((STEPS, PAIR))]
        + [pltpu.SemaphoreType.DMA((TAIL, PAIR))]
        + [pltpu.SemaphoreType.DMA((STEPS, PAIR))]
        + [pltpu.SemaphoreType.DMA((STEPS,))] * 2
        + [pltpu.SemaphoreType.DMA((TAIL,))]
        + [pltpu.SemaphoreType.DMA((7,))],
        compiler_params=pltpu.CompilerParams(
            collective_id=0, has_side_effects=True, vmem_limit_bytes=50 * 1024 * 1024
        ),
        name="butterfly",
    )(
        coeffs.reshape((RING, PAIR, TAIL) + block),
        row_weights.reshape((LEVELS, RING, PAIR, TAIL) + factor),
        col_weights.reshape((LEVELS, GROUP, TAIL) + factor),
    )
    return out.reshape(coeffs.shape)


def solution(mesh):
    return jax.shard_map(
        per_device,
        mesh=mesh,
        in_specs=(
            P("row", "col", None, None, None, None),
            P(None, "row", "col", None, None, None, None),
            P(None, "row", "col", None, None, None, None),
        ),
        out_specs=P("row", "col", None, None, None, None),
        check_vma=False,
    )
```

```python
import functools

import jax
import jax.numpy as jnp
from jax import lax
from jax.experimental import pallas as pl
from jax.experimental.pallas import tpu as pltpu
from jax.sharding import PartitionSpec as P

MESH = pl.DeviceIdType.MESH
RING = 4
PAIR = 2
GROUP = 8
TAIL = 8
R = 64
S = 512
PIECES = 4
WIDTH = S // PIECES
STEPS = TAIL * PIECES
LEVELS = 3


def split(value):
    high = value.astype(jnp.bfloat16)
    low = (value - high.astype(jnp.float32)).astype(jnp.bfloat16)
    return high, low


def product(weights, value):
    wh, wl = weights
    xh, xl = split(value)
    return jnp.dot(
        jnp.concatenate([wh, wl, wh], axis=1),
        jnp.concatenate([xh, xh, xl], axis=0),
        preferred_element_type=jnp.float32,
    )


def mix_pair(first, second, state, a, b):
    weights = split(jnp.concatenate([first, pltpu.roll(second, R, 1)], axis=0))
    y = product(weights, jnp.concatenate([state[a], state[b]], axis=0))
    state[a] = y[:R]
    state[b] = y[R:]


def mix_level(weights, state, stride):
    for a in range(state.shape[0]):
        if not a & stride:
            b = a | stride
            mix_pair(weights(a), weights(b), state, a, b)


def mix_own(weights, state, partner, a):
    state[a] = product(split(weights), jnp.concatenate([state[a], partner[a]], axis=0))


def kernel(
    x_ref, rw_ref, cw_ref, zb,
    xs, xp, xd, w0, wd, q, wb, x3, z4, cb,
    xs_in, xp_in, xd_in, xo_in, w0_in, wd_in, wo_in, q_in, wb_in, x3_in, z4_in, zb_in, cb_in,
    sent,
):
    row, column = lax.axis_index("row"), lax.axis_index("col")
    zl, y, core = row // GROUP, row // 2 % RING, row % 2
    x, zh = column // PAIR, column % PAIR
    near = 1 - zl
    far = 1 - zh

    def device(x, y, zh, zl):
        return (zl * GROUP + y * 2 + core, x * PAIR + zh)

    def remote(src, dst, kind, sem, there):
        pltpu.make_async_remote_copy(src, dst, sent.at[kind], sem, device_id=there, device_id_type=MESH).start()

    def local(src, dst, sem):
        pltpu.make_async_copy(src, dst, sem).start()

    def whole(ref, sem):
        pltpu.make_async_copy(ref, ref, sem).wait()

    barrier = pltpu.get_barrier_semaphore()
    partners = [device(x, y, zh, near)]
    for s in range(1, RING):
        partners += [device(x, (y + s) % RING, zh, zl), device((x + s) % RING, y, zh, zl)]
    partners += [device(x, y, far, side) for side in range(PAIR)]
    for there in partners:
        pl.semaphore_signal(barrier, 1, device_id=there, device_id_type=MESH)
    pl.semaphore_wait(barrier, len(partners))

    def place(n):
        return n // PIECES, n % PIECES

    def piece(n):
        t, part = place(n)
        return t, pl.ds(pl.multiple_of(part * WIDTH, WIDTH), WIDTH)

    def once(n, work):
        pl.when(place(n)[1] == 0)(work)

    def send0(n):
        t, cols = piece(n)
        remote(x_ref.at[:, zh, t, :, cols], xp.at[n], 0, xp_in.at[n], device(x, y, zh, near))
        local(x_ref.at[:, zh, t, :, cols], xs.at[n], xs_in.at[n])
        once(n, lambda: local(rw_ref.at[0, :, zh, t], w0.at[t], w0_in.at[t]))

    def send1(n):
        t, cols = piece(n)
        there = device(x, y, zh, near)
        for a in range(PAIR):
            mine = (x + PAIR * zl + a + t) % RING
            theirs = (x + PAIR * near + a + t) % RING

            @functools.partial(once, n)
            def _():
                remote(rw_ref.at[:, theirs, far, t], wd.at[t, PAIR + a], 1, wd_in.at[t], there)
                local(rw_ref.at[:, mine, far, t], wd.at[t, a], wo_in.at[t])

            remote(x_ref.at[theirs, far, t, :, cols], xd.at[n, PAIR + a], 0, xd_in.at[n], there)
            local(x_ref.at[mine, far, t, :, cols], xd.at[n, a], xo_in.at[n])

    def send_factor(src, dst, sem, s, yd):
        if s == 0:
            local(src, dst, sem)
        else:
            remote(src, dst, 2, sem, device(x, yd, zh, zl))

    def factor(n):
        t, _ = piece(n)

        @functools.partial(once, n)
        def _():
            local(cw_ref.at[:, :, t], cb.at[t], cb_in.at[t])
            for s in range(RING):
                yd = (y + s) % RING
                send_factor(rw_ref.at[pl.ds(1, 2), (x + yd + t) % RING, zh, t], wb.at[t, 0, y], wb_in.at[t, 0], s, yd)

    def across(t, side):
        return (zl + y // 2 + t + side) % 2

    def spread(src, dst, sem, s, yd):
        if s == 0:
            local(src, dst, sem)
        else:
            remote(src, dst, 3, sem, device(x, yd, zh, zl))

    def pair0(n):
        t, _ = piece(n)
        once(n, lambda: whole(w0.at[t], w0_in.at[t]))
        whole(xs.at[n], xs_in.at[n])
        whole(xp.at[n], xp_in.at[n])
        for a in range(RING):
            mix_own(w0[t, a], xs.at[n], xp.at[n], a)
        for s in range(RING):
            yd = (y + s) % RING
            spread(xs.at[n, (x + yd + t) % RING], q.at[n, 0, y], q_in.at[n, 0], s, yd)

    def pair1(n):
        t, _ = piece(n)

        @functools.partial(once, n)
        def _():
            whole(wd.at[t, pl.ds(0, PAIR)], wo_in.at[t])
            whole(wd.at[t, pl.ds(PAIR, PAIR)], wd_in.at[t])
            for s in range(RING):
                yd = (y + s) % RING
                e = (yd + PAIR * (t + zh)) % RING
                send_factor(wd.at[t, e, pl.ds(1, 2)], wb.at[t, 1, y], wb_in.at[t, 1], s, yd)

        whole(xd.at[n, pl.ds(0, PAIR)], xo_in.at[n])
        whole(xd.at[n, pl.ds(PAIR, PAIR)], xd_in.at[n])
        for a in range(PAIR):
            mix_pair(wd[t, a, 0], wd[t, PAIR + a, 0], xd.at[n], a, PAIR + a)
        for s in range(RING):
            yd = (y + s) % RING
            spread(xd.at[n, (yd + PAIR * (t + zh)) % RING], q.at[n, 1, y], q_in.at[n, 1], s, yd)

    def ring_step(n, part):
        t, _ = piece(n)
        once(n, lambda: whole(wb.at[t, part], wb_in.at[t, part]))
        whole(q.at[n, part], q_in.at[n, part])
        for level in range(2):
            mix_level(lambda a: wb[t, part, a, level], q.at[n, part], 2 >> level)
        shift = (y if part == 0 else PAIR * zl + y % 2) + t
        src, dst, sem = q.at[n, part], x3.at[n, part], x3_in.at[n, part]
        at_home = shift % RING == 0
        pl.when(at_home)(lambda: local(src, dst, sem))
        pl.when(jnp.logical_not(at_home))(
            lambda: remote(src, dst, 4, sem, device((x + shift) % RING, y, zh, zl))
        )

    def ring0(n):
        ring_step(n, 0)

    def ring1(n):
        ring_step(n, 1)

    def give_back(held, n, j):
        t, cols = piece(n)
        for s in range(RING):
            yi = (y + s) % RING
            src, dst = held.at[yi], zb.at[j, t, :, cols]
            if s == 0:
                local(src, dst, zb_in.at[n])
            else:
                remote(src, dst, 6, zb_in.at[n], device(x, yi, zh, zl))

    def turn1(n):
        t, _ = piece(n)
        whole(x3.at[n, 1], x3_in.at[n, 1])
        remote(x3.at[n, 1], z4.at[n], 5, z4_in.at[n], device(x, y, far, across(t, zh)))

    def back0(n):
        t, _ = piece(n)
        whole(x3.at[n, 0], x3_in.at[n, 0])
        give_back(x3.at[n, 0], n, PAIR * ((x - y - t + 16) % RING) + zh)

    def back1(n):
        t, _ = piece(n)
        whole(z4.at[n], z4_in.at[n])
        give_back(z4.at[n], n, PAIR * ((x - PAIR * across(t, far) - y % 2 - t + 16) % RING) + far)

    def col(n):
        t, cols = piece(n)
        once(n, lambda: whole(cb.at[t], cb_in.at[t]))
        state = zb.at[:, t, :, cols]
        whole(state, zb_in.at[n])
        for level in range(LEVELS):
            mix_level(lambda a: cb[t, level, a], state, GROUP >> level + 1)

    order = (
        (col, 25),
        (send1, 8),
        (back1, 20),
        (turn1, 16),
        (factor, 0),
        (back0, 19),
        (ring0, 17),
        (ring1, 13),
        (pair1, 11),
        (send0, 12),
        (pair0, 15),
    )
    last = max(lag for _, lag in order)

    def step(n, carry):
        for work, lag in order:
            pl.when((n >= lag) & (n < STEPS + lag))(functools.partial(work, n - lag))
        return carry

    lax.fori_loop(0, STEPS + last, step, 0)

    whole(xp, sent.at[0])
    whole(xd.at[:, pl.ds(0, PAIR)], sent.at[0])
    whole(wd.at[:, pl.ds(0, PAIR)], sent.at[1])
    whole(wb.at[:, :, pl.ds(0, RING - 1)], sent.at[2])
    whole(q.at[:, :, pl.ds(0, RING - 1)], sent.at[3])
    whole(x3.at[pl.ds(0, STEPS - STEPS // RING)], sent.at[4])
    whole(z4, sent.at[5])
    whole(zb.at[pl.ds(0, GROUP - PAIR)], sent.at[6])


def per_device(coeffs, row_weights, col_weights):
    block, factor, part = (R, S), (R, 2 * R), (R, WIDTH)
    buffers = [
        (STEPS, RING) + part,
        (STEPS, RING) + part,
        (STEPS, RING) + part,
        (TAIL, RING) + factor,
        (TAIL, RING, LEVELS) + factor,
        (STEPS, PAIR, RING) + part,
        (TAIL, PAIR, RING, LEVELS - 1) + factor,
        (STEPS, PAIR, RING) + part,
        (STEPS, RING) + part,
        (TAIL, LEVELS, GROUP) + factor,
    ]
    out = pl.pallas_call(
        kernel,
        out_shape=pltpu.VMEM((GROUP, TAIL) + block, jnp.float32),
        in_specs=[pl.BlockSpec(memory_space=pl.ANY)] * 3,
        out_specs=pl.BlockSpec(memory_space=pltpu.VMEM),
        scratch_shapes=[pltpu.VMEM(shape, jnp.float32) for shape in buffers]
        + [pltpu.SemaphoreType.DMA((STEPS,))] * 4
        + [pltpu.SemaphoreType.DMA((TAIL,))] * 3
        + [pltpu.SemaphoreType.DMA((STEPS, PAIR))]
        + [pltpu.SemaphoreType.DMA((TAIL, PAIR))]
        + [pltpu.SemaphoreType.DMA((STEPS, PAIR))]
        + [pltpu.SemaphoreType.DMA((STEPS,))] * 2
        + [pltpu.SemaphoreType.DMA((TAIL,))]
        + [pltpu.SemaphoreType.DMA((7,))],
        compiler_params=pltpu.CompilerParams(
            collective_id=0, has_side_effects=True, vmem_limit_bytes=50 * 1024 * 1024
        ),
        name="butterfly",
    )(
        coeffs.reshape((RING, PAIR, TAIL) + block),
        row_weights.reshape((LEVELS, RING, PAIR, TAIL) + factor),
        col_weights.reshape((LEVELS, GROUP, TAIL) + factor),
    )
    return out.reshape(coeffs.shape)


def solution(mesh):
    return jax.shard_map(
        per_device,
        mesh=mesh,
        in_specs=(
            P("row", "col", None, None, None, None),
            P(None, "row", "col", None, None, None, None),
            P(None, "row", "col", None, None, None, None),
        ),
        out_specs=P("row", "col", None, None, None, None),
        check_vma=False,
    )
```
